1024 devices in a mesh: section: 4 (over z_lo, core), rep: 4 (over z_hi), expert: 64 (over y, x).
Axes of the slice: x: 8, y: 8, z: 8 (z_hi: 4, z_lo: 2; z = z_hi * 2 + z_lo), core: 2. Of those that a mesh axis runs over, the one named last changes fastest.
Arguments:
- activations: bfloat16 [4, 4, 4096, 7168], P('section', 'rep', 'expert'), may hold values from -6 to 6
- routes: int32 [4, 4, 4096, 8], P('section', 'rep', 'expert'), may hold values from 0 to 255, all different within a row; in each aligned block of 64 rows (0 to 63, 64 to 127, ..., all dimensions but the last counted through in order) at most 2 rows name the same one
- gate_values: float32 [4, 4, 4096, 8], P('section', 'rep', 'expert'), may hold values from 0.1 to 1
- w_gate: bfloat16 [4, 7168, 8192], P('section', None, 'expert'), may hold values from -0.0625 to 0.0625
- w_up: bfloat16 [4, 7168, 8192], P('section', None, 'expert'), may hold values from -0.0625 to 0.0625
- w_down: bfloat16 [4, 8192, 7168], P('section', 'expert'), may hold values from -0.125 to 0.125
Outputs:
- handed: bfloat16 [4, 4, 4096, 7168], P('section', 'rep', 'expert')
- load_share: float32 [4, 4], P('section')
The draws below stay inside these ranges and needn't reach their ends.
Inputs may be any that keep to these rules, and one draw needn't show every extreme that they name: The 8 routes of a token name different experts; in each aligned block of 64 tokens (the tokens of one device) at most 2 tokens name one expert.
All inputs are finite; a program needn't handle non-finite values.
Results may differ from the reference program's by a relative error of at most 0.012.
Values may be sent and summed in bfloat16 or wider, within the bound.
A program may use at most 32 MiB of HBM per device.

```python
import math
import jax
import jax.numpy as jnp
import numpy as np
from jax import lax

D = 7168
HIDDEN_SIZE = 2048
ALL_EXPERTS = 256
TOP = 8
EXPERTS = 4
CAPACITY = 2
TOK_DEV = 64
TOKENS = 4096
SECTIONS = 4
REPS = 4
N_EXPERT = 64


def shard_levels(stream_key, shape, split, low, top_value):
    loudness, own = 1.0, jax.random.fold_in(stream_key, 6)
    for axis_at, shards_of in split:
        steps = jnp.exp(jax.random.uniform(jax.random.fold_in(own, axis_at), (shards_of,), jnp.float32, low / len(split), top_value / len(split)))
        loudness = loudness * jnp.repeat(steps, shape[axis_at] // shards_of).reshape([-1 if axis == axis_at else 1 for axis in range(len(shape))])
    return loudness


def deal_out(stream_key, own, number, rows, count, top, limit, lean):
    sequence = jax.random.permutation(stream_key, count)
    crowded, common = shares(count, rows * top, limit, lean, True), shares(count, rows * top, limit, lean, False)
    places = jnp.arange(count)

    def named(sizes, rotation):
        used = int((sizes > 0).sum())
        fixed = max(1, used // 4)
        moved = fixed + (places - fixed + rotation * (used - fixed)) % max(1, count - fixed)
        return jnp.zeros((count,), jnp.int32).at[sequence[jnp.where(places < fixed, places, moved)]].set(jnp.asarray(sizes, jnp.int32))

    sizes = jnp.where(number % 4 == 0, named(crowded, number // 4), named(common, number - number // 4 - 1))
    mixed = jax.random.permutation(jax.random.fold_in(own, 3), count)
    donor, taker = mixed[0:count // 2 * 2:2], mixed[1:count // 2 * 2:2]
    room = jnp.minimum(sizes[donor] - 1, limit - sizes[taker]) // 2
    room = jnp.where((donor == sequence[0]) | (taker == sequence[0]) | (sizes[taker] == 0), 0, jnp.maximum(room, 0))
    moved = jax.random.randint(jax.random.fold_in(own, 4), (count // 2,), 0, 1 << 20) % (room + 1)
    sizes = sizes.at[donor].add(-moved).at[taker].add(moved)
    items = jnp.searchsorted(jnp.cumsum(sizes), jnp.arange(rows * top), side="right").astype(jnp.int32)
    grid = items.reshape(top, rows).T
    grid = grid[jax.random.permutation(jax.random.fold_in(own, 1), rows)]
    rotation = jax.random.randint(jax.random.fold_in(own, 2), (rows, 1), 0, top)
    return jnp.take_along_axis(grid, (jnp.arange(top)[None, :] + rotation) % top, axis=1)


def shares(number_of, total, most, skew, full):
    weights = [(1 << 20) // math.isqrt(grade ** skew) + 1 for grade in range(1, number_of + 1)]
    largest = most if full else min(most, max(-(-total // number_of), total * weights[0] // sum(weights)))
    least = 1 if total - largest >= number_of - 1 else 0
    given, surplus = [largest] + [least] * (number_of - 1), total - largest - least * (number_of - 1)
    while surplus > 0:
        candidates = [i for i in range(1, number_of) if given[i] < largest] or [i for i in range(1, number_of) if given[i] < most]
        whole, budget = sum([weights[i] for i in candidates]), surplus
        for i in candidates:
            extra = min(most - given[i], max(1, budget * weights[i] // whole), surplus)
            given[i] = given[i] + extra
            surplus = surplus - extra
    return np.array(given)


def noise(own_key, dims, width, bound, shards=(), kind=jnp.bfloat16):
    loudness = shard_levels(own_key, dims, shards, -0.22, 0.18) if shards else 1.0
    array = jax.random.normal(own_key, dims, jnp.float32) * width * loudness
    return jnp.minimum(jnp.maximum(array, -bound), bound).astype(kind)


def setup_inputs(seed: int = 0) -> dict:
    seeds = jax.random.split(jax.random.key(seed), 7)
    activations = noise(seeds[0], (SECTIONS, REPS, TOKENS, D), 1.0, 6.0, ((0, 4), (1, 4), (2, 64)))
    routes_keys = jax.random.split(jax.random.fold_in(seeds[1], 1), SECTIONS * REPS * TOKENS // TOK_DEV)
    routes_turns = jax.random.permutation(jax.random.fold_in(seeds[1], 3), SECTIONS * REPS * TOKENS // TOK_DEV)
    routes = jax.vmap(lambda own, number: deal_out(jax.random.fold_in(seeds[1], 2), own, number, TOK_DEV, ALL_EXPERTS, TOP, CAPACITY, 2))(routes_keys, routes_turns).reshape((SECTIONS, REPS, TOKENS, TOP))
    gate_values = jnp.clip(jnp.exp(math.log(1.0) - 2.3025851 * jax.random.uniform(seeds[2], (SECTIONS, REPS, TOKENS, TOP), jnp.float32) ** shard_levels(seeds[2], (SECTIONS, REPS, TOKENS, TOP), ((0, 4), (1, 4), (2, 64)), -0.2, 0.2)), 0.1, 1.0)
    w_gate = noise(seeds[3], (SECTIONS, D, EXPERTS * HIDDEN_SIZE), D ** -0.5, 0.0625, ((0, 4), (2, 64)))
    w_up = noise(seeds[4], (SECTIONS, D, EXPERTS * HIDDEN_SIZE), D ** -0.5, 0.0625, ((0, 4), (2, 64)))
    w_down = noise(seeds[5], (SECTIONS, EXPERTS * HIDDEN_SIZE, D), HIDDEN_SIZE ** -0.5, 0.125, ((0, 4), (1, 64)))
    return {"activations": activations, "routes": routes, "gate_values": gate_values, "w_gate": w_gate, "w_up": w_up, "w_down": w_down}


def route_tables(route_ids, gates):
    expert_ids = jnp.arange(EXPERTS, dtype=jnp.int32)
    matches = (route_ids[:, :, None] == expert_ids[None, None, :]).astype(jnp.float32)
    hits = jnp.sum(matches, axis=1)
    mass = jnp.sum(gates.astype(jnp.float32)[:, :, None] * matches, axis=1)
    return hits, mass


def slot_picks(hits):
    before = jnp.cumsum(hits, axis=0) - hits
    slots = jnp.arange(CAPACITY).astype(jnp.float32)
    picks = hits[:, :, None] * (before[:, :, None] == slots[None, None, :]).astype(jnp.float32)
    return jnp.transpose(picks, (1, 2, 0))


def span_mix(acts, route_ids, gates, w_gate, w_up, w_down):
    tok_dev = acts.shape[0] // N_EXPERT
    members = N_EXPERT // EXPERTS
    slice_width = HIDDEN_SIZE // members
    highest = lax.Precision.HIGHEST
    hits, mass = route_tables(route_ids, gates)
    weights_b = mass.astype(jnp.bfloat16)
    picks = jax.vmap(slot_picks)(hits.reshape(N_EXPERT, tok_dev, EXPERTS))
    acts_blocks = acts.reshape(N_EXPERT, tok_dev, D).astype(jnp.float32)
    rows = jnp.einsum("bect,btd->ebcd", picks, acts_blocks, precision=highest).astype(jnp.bfloat16)
    rows = rows.reshape(EXPERTS, N_EXPERT * CAPACITY, D)
    weight_blocks = weights_b.reshape(N_EXPERT, tok_dev, EXPERTS).astype(jnp.float32)
    row_weights = jnp.einsum("bect,bte->ebc", picks, weight_blocks, precision=highest)
    row_weights = row_weights.reshape(EXPERTS, N_EXPERT * CAPACITY)

    def add_slice(slice_index, running):
        slice_index = jnp.asarray(slice_index).astype(jnp.int32)
        expert_now = (slice_index // members).astype(jnp.int32)
        begin = (slice_index * slice_width).astype(jnp.int32)
        rows_now = lax.dynamic_index_in_dim(rows, expert_now, 0, keepdims=False)
        weight_now = lax.dynamic_index_in_dim(row_weights, expert_now, 0, keepdims=False)
        gate_cols = lax.dynamic_slice_in_dim(w_gate, begin, slice_width, 1)
        up_cols = lax.dynamic_slice_in_dim(w_up, begin, slice_width, 1)
        down_rows = lax.dynamic_slice_in_dim(w_down, begin, slice_width, 0)
        gate_proj = jnp.dot(rows_now, gate_cols, preferred_element_type=jnp.float32)
        up_proj = jnp.dot(rows_now, up_cols, preferred_element_type=jnp.float32)
        hidden = (jax.nn.silu(gate_proj) * up_proj).astype(jnp.bfloat16)
        partial_out = jnp.dot(hidden, down_rows, preferred_element_type=jnp.float32)
        weighted = (weight_now[:, None] * partial_out).astype(jnp.bfloat16)
        weighted = lax.optimization_barrier(weighted)
        return running.at[expert_now].add(weighted.astype(jnp.float32))

    start_sum = jnp.zeros((EXPERTS, N_EXPERT * CAPACITY, D), jnp.float32)
    running = lax.fori_loop(0, N_EXPERT, add_slice, start_sum)
    running = running.reshape(EXPERTS, N_EXPERT, CAPACITY, D)
    mixed = jnp.einsum("bect,ebcd->btd", picks, running, precision=highest)
    return mixed.reshape(N_EXPERT * tok_dev, D).astype(jnp.bfloat16), jnp.sum(mass, axis=0)


def reference(activations, routes, gate_values, w_gate, w_up, w_down):
    def per_section(section_args):
        acts_section, routes_section, gates_section, gate_w, up_w, down_w = section_args

        def per_span(span_args):
            acts_span, routes_span, gates_span = span_args
            return span_mix(acts_span, routes_span, gates_span, gate_w, up_w, down_w)

        mixed_all, mass_all = lax.map(per_span, (acts_section, routes_section, gates_section))
        return mixed_all, jnp.sum(mass_all, axis=0)

    mixed, mass = lax.map(per_section, (activations, routes, gate_values, w_gate, w_up, w_down))
    handed = jnp.roll(mixed, 1, axis=0)
    load_share = mass / jnp.float32(REPS * TOKENS)
    return handed, load_share
```

```python
import functools

import jax
import jax.numpy as jnp
from jax import lax
from jax.experimental import pallas as pl
from jax.experimental.pallas import tpu as pltpu
from jax.sharding import PartitionSpec as P

MESH = pl.DeviceIdType.MESH
BF16 = jnp.bfloat16
F32 = jnp.float32
EXPERTS = 4
N = 8
HALF = N // 2
UNIT = 1024
LANES = 128


def iota(shape, axis):
    return lax.broadcasted_iota(jnp.int32, shape, axis)


def dot(a, b):
    return jnp.dot(a, b, preferred_element_type=F32)


def one_hot(mask):
    return jnp.where(mask, 1.0, 0.0).astype(BF16)


def routing(routes_ref, gates_ref):
    tokens = routes_ref.shape[1]
    rows = EXPERTS * 2 * 8
    row = iota((rows, tokens), 0)
    expert = lax.div(row, 16)
    slot = lax.rem(lax.div(row, 8), 2).astype(F32)
    hits = jnp.zeros((rows, tokens), F32)
    mass = jnp.zeros((rows, tokens), F32)
    for k in range(routes_ref.shape[0]):
        same = routes_ref[k : k + 1, :] == expert
        hits = hits + jnp.where(same, 1.0, 0.0)
        mass = mass + jnp.where(same, gates_ref[k : k + 1, :], 0.0)
    earlier = one_hot(iota((tokens, tokens), 0) < iota((tokens, tokens), 1))
    before = dot(hits.astype(BF16), earlier)
    picks = jnp.where(before == slot, hits, 0.0)
    return picks, mass


def expert_mass(routes_ref, gates_ref):
    tokens = routes_ref.shape[1]
    expert = iota((8, tokens), 0)
    mass = jnp.zeros((8, tokens), F32)
    for k in range(routes_ref.shape[0]):
        same = routes_ref[k : k + 1, :] == expert
        mass = mass + jnp.where(same, gates_ref[k : k + 1, :], 0.0)
    return jnp.broadcast_to(jnp.sum(mass, axis=1, keepdims=True), (8, LANES))


def layer_kernel(
    sizes,
    routes_ref, gates_ref, acts_hbm, gate_hbm, up_hbm, down_hbm,
    own_ref, both_ref, pw_ref, load_ref,
    acts, w_in, w_out, picked, first_own, first_both, rows, pw_out,
    mass_out, mass_y, mass_x, mass_z,
    part, rung, send_own, send_both, got_own, got_both, last_own, last_both,
    load_sem, pw_sem, my_sem, mx_sem, mz_sem, fo_sem, fb_sem,
    go_sem, gb_sem, gr_sem, rr_sem, so_sem, sb_sem, lo_sem, lb_sem,
):
    sections, reps, own_units, both_units = sizes
    own_w, both_w = own_units * UNIT, both_units * UNIT
    tokens = acts.shape[0]
    section, rep, index = (lax.axis_index(a) for a in ("section", "rep", "expert"))
    x, y = lax.rem(index, N), lax.div(index, N)
    expert, side = lax.div(y, 2), lax.rem(y, 2)

    def at(x_, y_):
        return {"expert": lax.rem(y_ + N, N) * N + lax.rem(x_ + N, N)}

    def block(d):
        return lax.rem(x + d + N, N)

    def remote(src, dst, sems, i, device):
        return pltpu.make_async_remote_copy(
            src_ref=src, dst_ref=dst, send_sem=sems.at[(0, *i)], recv_sem=sems.at[(1, *i)],
            device_id=device, device_id_type=MESH,
        )

    sent = []

    def start(copy):
        copy.start()
        sent.append(copy)
        return copy

    loads = [
        pltpu.make_async_copy(acts_hbm, acts, load_sem.at[0]),
        pltpu.make_async_copy(gate_hbm, w_in.at[:, 0:LANES], load_sem.at[1]),
        pltpu.make_async_copy(up_hbm, w_in.at[:, LANES : 2 * LANES], load_sem.at[2]),
        pltpu.make_async_copy(down_hbm, w_out, load_sem.at[3]),
    ]
    for load in loads:
        load.start()

    ahead = {"section": lax.rem(section + 1, sections)}
    behind = {"section": lax.rem(section + sections - 1, sections)}
    barrier = pltpu.get_barrier_semaphore()
    for d in range(1, N):
        for device in (at(x, y + d - N), at(x + d - N, y)):
            pl.semaphore_signal(barrier, inc=1, device_id=device, device_id_type=MESH)
    for d in range(1, reps):
        pl.semaphore_signal(barrier, inc=1, device_id={"rep": lax.rem(rep + d, reps)}, device_id_type=MESH)
    for d in range(N):
        pl.semaphore_signal(barrier, inc=1, device_id={**behind, **at(x, y + d - N)}, device_id_type=MESH)

    picks, mass = routing(routes_ref, gates_ref)
    pw_out[...] = jnp.where(picks > 0, mass, 0.0).astype(BF16)
    mass_out[0] = expert_mass(routes_ref, gates_ref)
    spread = one_hot(iota((tokens, 8 * tokens), 0) == lax.rem(iota((tokens, 8 * tokens), 1), tokens))
    wide = dot(picks.astype(BF16), spread)
    wide_rows, wide_cols = iota(wide.shape, 0), iota(wide.shape, 1)
    wide = jnp.where(lax.rem(wide_rows, 8) == lax.div(wide_cols, tokens), wide, 0.0).astype(BF16)
    loads[0].wait()

    def pick_unit(u):
        stacked = jnp.concatenate(
            [acts[:, u * UNIT + i * LANES : u * UNIT + (i + 1) * LANES] for i in range(8)], axis=0
        )
        picked[:, u] = dot(wide, stacked).astype(BF16).reshape(EXPERTS, 16, LANES)

    for u in (*range(own_units), *range(own_units + both_units, 2 * own_units + both_units)):
        pick_unit(u)
    pl.semaphore_wait(barrier, (N - 1) * 2 + (reps - 1) + N)

    own_copies, both_copies, mass_copies = [], [], []
    for d in range(1, N):
        to_y = lax.rem(y + d, N)
        own_copies.append(start(remote(
            picked.at[lax.div(to_y, 2), pl.ds(lax.rem(to_y, 2) * (own_units + both_units), own_units)],
            first_own.at[y], fo_sem, (d,), at(x, to_y),
        )))
    first_own[y] = picked[expert, pl.ds(side * (own_units + both_units), own_units)]
    for u in range(own_units, own_units + both_units):
        pick_unit(u)
    for d in range(1, N):
        to_y = lax.rem(y + d, N)
        both_copies.append(start(remote(
            picked.at[lax.div(to_y, 2), pl.ds(own_units, both_units)],
            first_both.at[y], fb_sem, (d,), at(x, to_y),
        )))
    first_both[y] = picked[expert, pl.ds(own_units, both_units)]
    pw_copy = start(remote(pw_out, pw_ref, pw_sem, (), {**ahead}))
    for d in range(1, N):
        mass_copies.append(start(remote(mass_out.at[0], mass_y.at[y], my_sem, (d,), at(x, y + d - N))))
    mass_y[y] = mass_out[0]

    perm_rows, perm_cols = iota((128, 128), 0), iota((128, 128), 1)

    def inner(k):
        return lax.rem(lax.div(k, 2), 8) * 16 + lax.rem(k, 2) * 8 + lax.div(k, 16)

    gather_perm = one_hot(perm_cols == inner(perm_rows))
    scatter_perm = one_hot(perm_rows == inner(perm_cols))

    def assemble(buf, k):
        mixed = dot(gather_perm, buf[:, k].reshape(128, LANES)).astype(BF16)
        return jnp.concatenate([mixed[i * 16 : (i + 1) * 16] for i in range(8)], axis=1)

    def own_cols(first=0, width=own_w, mine=True):
        which = side if mine else 1 - side
        return pl.ds(pl.multiple_of(which * (own_w + both_w) + first, LANES), width)

    def both_cols(first=0, width=both_w):
        return pl.ds(own_w + first, width)

    def gather_copy(is_own, way, hop):
        sign = 1 if way == 0 else -1
        width = own_w if is_own else both_w
        first = 0
        if hop == HALF:
            width //= 2
            first = way * width
        cols = own_cols(first, width) if is_own else both_cols(first, width)
        piece = rows.at[block(-sign * (hop - 1)), :, cols]
        return remote(piece, piece, go_sem if is_own else gb_sem, (way, hop - 1), at(x + sign, y))

    def rung_copy(i, d, first=0, width=own_w):
        piece = rows.at[block(d), :, own_cols(first, width)]
        return remote(piece, piece, gr_sem, (i,), at(x, y + 1 - 2 * side))

    gathers = {}
    rungs = []
    for copy in own_copies:
        copy.wait_recv()
    for k in range(own_units):
        rows[x, :, own_cols(k * UNIT, UNIT)] = assemble(first_own, k)
    for way in range(2):
        gathers[True, way, 1] = start(gather_copy(True, way, 1))
    rungs.append(start(rung_copy(0, 0)))
    for copy in both_copies:
        copy.wait_recv()
    for k in range(both_units):
        rows[x, :, both_cols(k * UNIT, UNIT)] = assemble(first_both, k)
    for way in range(2):
        gathers[False, way, 1] = start(gather_copy(False, way, 1))

    for copy in mass_copies:
        copy.wait_recv()
    mass_out[1] = functools.reduce(jnp.add, [mass_y[i] for i in range(N)])
    mass_x[x] = mass_out[1]
    mass_copies = [
        start(remote(mass_out.at[1], mass_x.at[x], mx_sem, (d,), at(x + d - N, y))) for d in range(1, N)
    ]

    for hop in range(1, HALF):
        for is_own in (True, False):
            for way in range(2):
                gathers[is_own, way, hop].wait_recv()
                gathers[is_own, way, hop + 1] = start(gather_copy(is_own, way, hop + 1))
                if is_own:
                    rungs.append(start(rung_copy(len(rungs), (-1 if way == 0 else 1) * hop)))
        if hop == 1:
            for copy in mass_copies:
                copy.wait_recv()
            mass_out[2] = functools.reduce(jnp.add, [mass_x[i] for i in range(N)])
            mass_z[rep] = mass_out[2]
            mass_copies = [
                start(remote(mass_out.at[2], mass_z.at[rep], mz_sem, (d,), {"rep": lax.rem(rep + d, reps)}))
                for d in range(1, reps)
            ]
    for way in range(2):
        gathers[True, way, HALF].wait_recv()
        width = own_w // 2
        rungs.append(start(rung_copy(len(rungs), HALF, way * width, width)))

    step = 512

    def project(total, first, width):
        def body(j, total):
            cols = pl.ds(pl.multiple_of(first + j * step, step), step)
            return total + dot(rows[:, :, cols].reshape(128, step), w_in[cols, :])

        return lax.fori_loop(0, width // step, body, total)

    loads[1].wait()
    loads[2].wait()
    total = project(jnp.zeros((128, 2 * LANES), F32), side * (own_w + both_w), own_w)
    for way in range(2):
        gathers[False, way, HALF].wait_recv()
    total = project(total, own_w, both_w)
    for copy in rungs:
        copy.wait_recv()
    total = project(total, (1 - side) * (own_w + both_w), own_w)
    gate, up = total[:, :LANES], total[:, LANES:]
    hidden = (gate / (1.0 + jnp.exp(-gate)) * up).astype(BF16)
    loads[3].wait()

    def down(first, width):
        def body(j, carry):
            cols = pl.ds(pl.multiple_of(first + j * step, step), step)
            part[:, :, cols] = dot(hidden, w_out[:, cols]).astype(BF16).reshape(N, 16, step)
            return carry

        lax.fori_loop(0, width // step, body, 0)

    order = [HALF]
    for d in range(HALF - 1, 0, -1):
        order += [d, -d]
    order.append(0)
    down((1 - side) * (own_w + both_w), own_w)
    over = {}
    for i, d in enumerate(order):
        over[d] = start(remote(
            part.at[block(d), :, own_cols(mine=False)], rung.at[block(d)], rr_sem, (i,), at(x, y + 1 - 2 * side),
        ))

    def scatter_copy(is_own, way, hop, src):
        dst = (got_own if is_own else got_both).at[way, hop - 1]
        if hop == 1:
            dst = dst.at[:, 0 : (own_w if is_own else both_w) // 2]
        return remote(src, dst, so_sem if is_own else sb_sem, (way, hop - 1), at(x + 1 - 2 * way, y))

    scatters = {}
    down(own_w, both_w)
    for way in range(2):
        src = part.at[block(HALF), :, both_cols(way * (both_w // 2), both_w // 2)]
        scatters[False, way, 1] = start(scatter_copy(False, way, 1, src))
    down(side * (own_w + both_w), own_w)

    def mine(is_own, d):
        if is_own:
            return part[block(d), :, own_cols()].astype(F32) + rung[block(d)].astype(F32)
        return part[block(d), :, both_cols()].astype(F32)

    over[HALF].wait_recv()
    send_own[0, 0] = mine(True, HALF).astype(BF16)
    for way in range(2):
        src = send_own.at[0, 0, :, way * (own_w // 2) : (way + 1) * (own_w // 2)]
        scatters[True, way, 1] = start(scatter_copy(True, way, 1, src))
    for hop in range(2, HALF + 1):
        for is_own in (False, True):
            send, got = (send_own, got_own) if is_own else (send_both, got_both)
            width = own_w if is_own else both_w
            for way in range(2):
                d = (1 - 2 * way) * (HALF + 1 - hop)
                if is_own:
                    over[d].wait_recv()
                scatters[is_own, way, hop - 1].wait_recv()
                value = mine(is_own, d)
                if hop == 2:
                    left, right = way * (width // 2), (way + 1) * (width // 2)
                    came = got[way, 0, :, 0 : width // 2].astype(F32)
                    halves = [value[:, : width // 2], value[:, width // 2 :]]
                    halves[way] = halves[way] + came
                    value = jnp.concatenate(halves, axis=1)
                else:
                    value = value + got[way, hop - 2].astype(F32)
                send[way, hop - 1] = value.astype(BF16)
                scatters[is_own, way, hop] = start(scatter_copy(is_own, way, hop, send.at[way, hop - 1]))

    last_copies = []
    for is_own in (False, True):
        got, last, landing, sems = (
            (got_own, last_own, own_ref, lo_sem) if is_own else (got_both, last_both, both_ref, lb_sem)
        )
        if is_own:
            over[0].wait_recv()
        for way in range(2):
            scatters[is_own, way, HALF].wait_recv()
        value = mine(is_own, 0)
        for way in range(2):
            value = value + got[way, HALF - 1].astype(F32)
        value = value.astype(BF16)
        for k in range(own_units if is_own else both_units):
            stacked = jnp.concatenate(
                [value[:, k * UNIT + i * LANES : k * UNIT + (i + 1) * LANES] for i in range(8)], axis=0
            )
            last[:, k] = dot(scatter_perm, stacked).astype(BF16).reshape(N, 16, LANES)
        for d in range(N):
            to_y = lax.rem(y + d, N)
            last_copies.append(start(remote(
                last.at[to_y], landing.at[expert, side], sems, (d,), {**ahead, **at(x, to_y)},
            )))

    for copy in mass_copies:
        copy.wait_recv()
    load_ref[...] = functools.reduce(jnp.add, [mass_z[i] for i in range(reps)])
    pw_copy.wait_recv()
    for copy in last_copies:
        copy.wait_recv()
    for copy in sent:
        copy.wait_send()


def spread_kernel(own_units, both_units, count, own_ref, both_ref, pw_ref, load_ref, out_ref, share_ref):
    tokens = pw_ref.shape[1]
    spread = one_hot(iota((8 * tokens, tokens), 1) == lax.rem(iota((8 * tokens, tokens), 0), tokens))
    wide = lax.dot_general(spread, pw_ref[...], (((1,), (1,)), ((), ())), preferred_element_type=F32)
    wide_rows, wide_cols = iota(wide.shape, 0), iota(wide.shape, 1)
    wide = jnp.where(lax.rem(wide_cols, 8) == lax.div(wide_rows, tokens), wide, 0.0).astype(BF16)
    for u in range(2 * own_units + both_units):
        if u < own_units:
            value = own_ref[:, 0, u].astype(F32)
        elif u < own_units + both_units:
            value = both_ref[:, 0, u - own_units].astype(F32) + both_ref[:, 1, u - own_units].astype(F32)
        else:
            value = own_ref[:, 1, u - own_units - both_units].astype(F32)
        value = value.reshape(EXPERTS * 16, LANES)
        high = value.astype(BF16)
        low = (value - high.astype(F32)).astype(BF16)
        both = dot(wide, jnp.concatenate([high, low], axis=1))
        both = (both[:, :LANES] + both[:, LANES:]).astype(BF16)
        for i in range(8):
            out_ref[:, u * UNIT + i * LANES : u * UNIT + (i + 1) * LANES] = both[i * tokens : (i + 1) * tokens]
    lane, row = iota((8, LANES), 1), iota((8, LANES), 0)
    picked = jnp.sum(jnp.where(lane == row, load_ref[...], 0.0), axis=0, keepdims=True)
    share_ref[...] = picked[:, :EXPERTS] / count


def local(activations, routes, gate_values, w_gate, w_up, w_down):
    acts = activations[0, 0]
    tokens, width = acts.shape
    sections, reps = lax.axis_size("section"), lax.axis_size("rep")
    own_units = width // UNIT * 2 // 7
    both_units = width // UNIT - 2 * own_units
    own_w, both_w = own_units * UNIT, both_units * UNIT
    vmem = pl.BlockSpec(memory_space=pltpu.VMEM)
    hbm = pl.BlockSpec(memory_space=pl.ANY)
    dma = pltpu.SemaphoreType.DMA
    outs = pl.pallas_call(
        functools.partial(layer_kernel, (sections, reps, own_units, both_units)),
        out_shape=(
            jax.ShapeDtypeStruct((EXPERTS, 2, own_units, 16, LANES), BF16),
            jax.ShapeDtypeStruct((EXPERTS, 2, both_units, 16, LANES), BF16),
            jax.ShapeDtypeStruct((EXPERTS * 16, tokens), BF16),
            jax.ShapeDtypeStruct((8, LANES), F32),
        ),
        in_specs=[vmem, vmem, hbm, hbm, hbm, hbm],
        out_specs=(vmem, vmem, vmem, vmem),
        scratch_shapes=[
            pltpu.VMEM((tokens, width), BF16),
            pltpu.VMEM((width, 2 * LANES), BF16),
            pltpu.VMEM((LANES, width), BF16),
            pltpu.VMEM((EXPERTS, 2 * own_units + both_units, 16, LANES), BF16),
            pltpu.VMEM((N, own_units, 16, LANES), BF16),
            pltpu.VMEM((N, both_units, 16, LANES), BF16),
            pltpu.VMEM((N, 16, width), BF16),
            pltpu.VMEM((EXPERTS * 16, tokens), BF16),
            pltpu.VMEM((3, 8, LANES), F32),
            pltpu.VMEM((N, 8, LANES), F32),
            pltpu.VMEM((N, 8, LANES), F32),
            pltpu.VMEM((reps, 8, LANES), F32),
            pltpu.VMEM((N, 16, width), BF16),
            pltpu.VMEM((N, 16, own_w), BF16),
            pltpu.VMEM((2, HALF, 16, own_w), BF16),
            pltpu.VMEM((2, HALF, 16, both_w), BF16),
            pltpu.VMEM((2, HALF, 16, own_w), BF16),
            pltpu.VMEM((2, HALF, 16, both_w), BF16),
            pltpu.VMEM((N, own_units, 16, LANES), BF16),
            pltpu.VMEM((N, both_units, 16, LANES), BF16),
            dma((4,)),
            dma((2,)),
            dma((2, N)),
            dma((2, N)),
            dma((2, reps)),
            dma((2, N)),
            dma((2, N)),
            dma((2, 2, HALF)),
            dma((2, 2, HALF)),
            dma((2, N + 1)),
            dma((2, N)),
            dma((2, 2, HALF)),
            dma((2, 2, HALF)),
            dma((2, N)),
            dma((2, N)),
        ],
        compiler_params=pltpu.CompilerParams(
            collective_id=0, has_side_effects=True, vmem_limit_bytes=48 * 2**20
        ),
        name="layer",
    )(routes[0, 0].T, gate_values[0, 0].T, acts, w_gate[0], w_up[0], w_down[0])
    count = float(reps * lax.axis_size("expert") * tokens)
    handed, share = pl.pallas_call(
        functools.partial(spread_kernel, own_units, both_units, count),
        out_shape=(
            jax.ShapeDtypeStruct((tokens, width), BF16),
            jax.ShapeDtypeStruct((1, EXPERTS), F32),
        ),
        in_specs=[vmem] * 4,
        out_specs=(vmem, vmem),
        name="spread",
    )(*outs)
    return handed[None, None], share


def solution(mesh):
    placed = (
        P("section", "rep", "expert", None),
        P("section", "rep", "expert", None),
        P("section", "rep", "expert", None),
        P("section", None, "expert"),
        P("section", None, "expert"),
        P("section", "expert", None),
    )
    return jax.shard_map(
        local,
        mesh=mesh,
        in_specs=placed,
        out_specs=(P("section", "rep", "expert", None), P("section", None)),
        check_vma=False,
    )
```

```python
import functools

import jax
import jax.numpy as jnp
from jax import lax
from jax.experimental import pallas as pl
from jax.experimental.pallas import tpu as pltpu
from jax.sharding import PartitionSpec as P

MESH = pl.DeviceIdType.MESH
BF16 = jnp.bfloat16
F32 = jnp.float32
EXPERTS = 4
N = 8
HALF = N // 2
UNIT = 1024
LANES = 128


def iota(shape, axis):
    return lax.broadcasted_iota(jnp.int32, shape, axis)


def dot(a, b):
    return jnp.dot(a, b, preferred_element_type=F32)


def one_hot(mask):
    return jnp.where(mask, 1.0, 0.0).astype(BF16)


def routing(routes_ref, gates_ref):
    tokens = routes_ref.shape[1]
    rows = EXPERTS * 2 * 8
    row = iota((rows, tokens), 0)
    expert = lax.div(row, 16)
    slot = lax.rem(lax.div(row, 8), 2).astype(F32)
    hits = jnp.zeros((rows, tokens), F32)
    mass = jnp.zeros((rows, tokens), F32)
    for k in range(routes_ref.shape[0]):
        same = routes_ref[k : k + 1, :] == expert
        hits = hits + jnp.where(same, 1.0, 0.0)
        mass = mass + jnp.where(same, gates_ref[k : k + 1, :], 0.0)
    earlier = one_hot(iota((tokens, tokens), 0) < iota((tokens, tokens), 1))
    before = dot(hits.astype(BF16), earlier)
    picks = jnp.where(before == slot, hits, 0.0)
    return picks, mass


def expert_mass(routes_ref, gates_ref):
    tokens = routes_ref.shape[1]
    expert = iota((8, tokens), 0)
    mass = jnp.zeros((8, tokens), F32)
    for k in range(routes_ref.shape[0]):
        same = routes_ref[k : k + 1, :] == expert
        mass = mass + jnp.where(same, gates_ref[k : k + 1, :], 0.0)
    return jnp.broadcast_to(jnp.sum(mass, axis=1, keepdims=True), (8, LANES))


def layer_kernel(
    sizes,
    routes_hbm, gates_hbm, acts_hbm, gate_hbm, up_hbm, down_hbm,
    own_ref, both_ref, pw_ref, mass_z,
    routes_ref, gates_ref,
    acts, w_in, w_out, picked, first_own, first_both, rows, pw_out,
    mass_out, mass_y, mass_x,
    part, rung, send_own, send_both, got_own, got_both, last_own, last_both,
    load_sem, pw_sem, my_sem, mx_sem, mz_sem, fo_sem, fb_sem,
    g_sem, gr_sem, rr_sem, s_sem, lo_sem, lb_sem, keep_sem,
):
    sections, reps, own_units, both_units, pieces = sizes
    own_w, both_w = own_units * UNIT, both_units * UNIT
    tokens = acts.shape[0]
    section, rep, index = (lax.axis_index(a) for a in ("section", "rep", "expert"))
    x, y = lax.rem(index, N), lax.div(index, N)
    expert, side = lax.div(y, 2), lax.rem(y, 2)

    def at(x_, y_):
        return {"expert": lax.rem(y_ + N, N) * N + lax.rem(x_ + N, N)}

    def block(d):
        return lax.rem(x + d + N, N)

    def remote(src, dst, sems, i, device):
        return pltpu.make_async_remote_copy(
            src_ref=src, dst_ref=dst, send_sem=sems.at[(0, *i)], recv_sem=sems.at[(1, *i)],
            device_id=device, device_id_type=MESH,
        )

    sent = []

    def start(copy):
        copy.start()
        sent.append(copy)
        return copy

    def finish():
        for copy in sent:
            copy.wait_send()

    loads = [
        pltpu.make_async_copy(routes_hbm, routes_ref, load_sem.at[0]),
        pltpu.make_async_copy(gates_hbm, gates_ref, load_sem.at[1]),
        pltpu.make_async_copy(acts_hbm, acts, load_sem.at[2]),
        pltpu.make_async_copy(gate_hbm, w_in.at[:, 0:LANES], load_sem.at[3]),
        pltpu.make_async_copy(up_hbm, w_in.at[:, LANES : 2 * LANES], load_sem.at[4]),
        pltpu.make_async_copy(down_hbm, w_out, load_sem.at[5]),
    ]
    for load in loads:
        load.start()

    ahead = {"section": lax.rem(section + 1, sections)}
    behind = {"section": lax.rem(section + sections - 1, sections)}
    barrier = pltpu.get_barrier_semaphore()
    for d in range(1, N):
        for device in (at(x, y + d - N), at(x + d - N, y)):
            pl.semaphore_signal(barrier, inc=1, device_id=device, device_id_type=MESH)
    for d in range(1, reps):

        @pl.when(rep + d < reps)
        def _():
            pl.semaphore_signal(barrier, inc=1, device_id={"rep": rep + d}, device_id_type=MESH)

    for d in range(N):
        pl.semaphore_signal(barrier, inc=1, device_id={**behind, **at(x, y + d - N)}, device_id_type=MESH)

    loads[0].wait()
    loads[1].wait()
    picks, mass = routing(routes_ref, gates_ref)
    pw_out[...] = jnp.where(picks > 0, mass, 0.0).astype(BF16)
    mass_out[0] = expert_mass(routes_ref, gates_ref)
    spread = one_hot(iota((tokens, 8 * tokens), 0) == lax.rem(iota((tokens, 8 * tokens), 1), tokens))
    wide = dot(picks.astype(BF16), spread)
    wide_rows, wide_cols = iota(wide.shape, 0), iota(wide.shape, 1)
    wide = jnp.where(lax.rem(wide_rows, 8) == lax.div(wide_cols, tokens), wide, 0.0).astype(BF16)
    loads[2].wait()

    def pick_unit(u):
        stacked = jnp.concatenate(
            [acts[:, u * UNIT + i * LANES : u * UNIT + (i + 1) * LANES] for i in range(8)], axis=0
        )
        picked[:, u] = dot(wide, stacked).astype(BF16).reshape(EXPERTS, 16, LANES)

    for u in (*range(own_units), *range(own_units + both_units, 2 * own_units + both_units)):
        pick_unit(u)
    pl.semaphore_wait(barrier, (N - 1) * 2 + N + rep)

    own_copies, both_copies, mass_copies = [], [], []
    for d in range(1, N):
        to_y = lax.rem(y + d, N)
        own_copies.append(start(remote(
            picked.at[lax.div(to_y, 2), pl.ds(lax.rem(to_y, 2) * (own_units + both_units), own_units)],
            first_own.at[y], fo_sem, (d,), at(x, to_y),
        )))
    first_own[y] = picked[expert, pl.ds(side * (own_units + both_units), own_units)]
    for u in range(own_units, own_units + both_units):
        pick_unit(u)
    for d in range(1, N):
        to_y = lax.rem(y + d, N)
        both_copies.append(start(remote(
            picked.at[lax.div(to_y, 2), pl.ds(own_units, both_units)],
            first_both.at[y], fb_sem, (d,), at(x, to_y),
        )))
    first_both[y] = picked[expert, pl.ds(own_units, both_units)]
    pw_copy = start(remote(pw_out, pw_ref, pw_sem, (), {**ahead}))
    for d in range(1, N):
        mass_copies.append(start(remote(mass_out.at[0], mass_y.at[y], my_sem, (d,), at(x, y + d - N))))
    mass_y[y] = mass_out[0]

    perm_rows, perm_cols = iota((128, 128), 0), iota((128, 128), 1)

    def inner(k):
        return lax.rem(lax.div(k, 2), 8) * 16 + lax.rem(k, 2) * 8 + lax.div(k, 16)

    gather_perm = one_hot(perm_cols == inner(perm_rows))
    scatter_perm = one_hot(perm_rows == inner(perm_cols))

    def assemble(buf, k):
        mixed = dot(gather_perm, buf[:, k].reshape(128, LANES)).astype(BF16)
        return jnp.concatenate([mixed[i * 16 : (i + 1) * 16] for i in range(8)], axis=1)

    def own_cols(first=0, width=own_w, mine=True):
        which = side if mine else 1 - side
        return pl.ds(pl.multiple_of(which * (own_w + both_w) + first, LANES), width)

    def both_cols(first=0, width=both_w):
        return pl.ds(own_w + first, width)

    def piece_cols(piece, first=0, width=None):
        is_own, start_, width_ = pieces[piece]
        cols = own_cols if is_own else both_cols
        return cols(start_ + first, width or width_)

    own_pieces = [i for i, piece in enumerate(pieces) if piece[0]]

    def gather_copy(piece, way, hop):
        sign = 1 if way == 0 else -1
        width = pieces[piece][2]
        first = 0
        if hop == HALF:
            width //= 2
            first = way * width
        ref = rows.at[block(-sign * (hop - 1)), :, piece_cols(piece, first, width)]
        return remote(ref, ref, g_sem, (piece, way, hop - 1), at(x + sign, y))

    def rung_copy(i, d, piece, first=0, width=None):
        ref = rows.at[block(d), :, piece_cols(piece, first, width)]
        return remote(ref, ref, gr_sem, (i,), at(x, y + 1 - 2 * side))

    gathers = {}
    rungs = []
    for copy in own_copies:
        copy.wait_recv()
    for k in range(own_units):
        rows[x, :, own_cols(k * UNIT, UNIT)] = assemble(first_own, k)
    for piece in own_pieces:
        for way in range(2):
            gathers[piece, way, 1] = start(gather_copy(piece, way, 1))
        rungs.append(start(rung_copy(len(rungs), 0, piece)))
    for copy in both_copies:
        copy.wait_recv()
    for k in range(both_units):
        rows[x, :, both_cols(k * UNIT, UNIT)] = assemble(first_both, k)
    for piece in range(len(pieces)):
        if piece not in own_pieces:
            for way in range(2):
                gathers[piece, way, 1] = start(gather_copy(piece, way, 1))

    def mass_copy(i, d):
        return remote(mass_out.at[2], mass_z.at[rep], mz_sem, (i,), {"rep": rep + d})

    keep = pltpu.make_async_copy(mass_out.at[2], mass_z.at[rep], keep_sem)

    for copy in mass_copies:
        copy.wait_recv()
    mass_out[1] = functools.reduce(jnp.add, [mass_y[i] for i in range(N)])
    mass_x[x] = mass_out[1]
    mass_copies = [
        start(remote(mass_out.at[1], mass_x.at[x], mx_sem, (d,), at(x + d - N, y))) for d in range(1, N)
    ]

    for hop in range(1, HALF):
        for piece in range(len(pieces)):
            for way in range(2):
                gathers[piece, way, hop].wait_recv()
                gathers[piece, way, hop + 1] = start(gather_copy(piece, way, hop + 1))
                if piece in own_pieces:
                    rungs.append(start(rung_copy(len(rungs), (-1 if way == 0 else 1) * hop, piece)))
        if hop == 1:
            for copy in mass_copies:
                copy.wait_recv()
            mass_out[2] = functools.reduce(jnp.add, [mass_x[i] for i in range(N)])
            keep.start()
            for d in range(1, reps):

                @pl.when(rep - d >= 0)
                def _():
                    mass_copy(d, -d).start()

    for piece in own_pieces:
        for way in range(2):
            gathers[piece, way, HALF].wait_recv()
            width = pieces[piece][2] // 2
            rungs.append(start(rung_copy(len(rungs), HALF, piece, way * width, width)))

    step = 512

    def project(total, first, width):
        def body(j, total):
            cols = pl.ds(pl.multiple_of(first + j * step, step), step)
            return total + dot(rows[:, :, cols].reshape(128, step), w_in[cols, :])

        return lax.fori_loop(0, width // step, body, total)

    loads[3].wait()
    loads[4].wait()
    total = project(jnp.zeros((128, 2 * LANES), F32), side * (own_w + both_w), own_w)
    for piece in range(len(pieces)):
        if piece not in own_pieces:
            for way in range(2):
                gathers[piece, way, HALF].wait_recv()
    total = project(total, own_w, both_w)
    for copy in rungs:
        copy.wait_recv()
    total = project(total, (1 - side) * (own_w + both_w), own_w)
    gate, up = total[:, :LANES], total[:, LANES:]
    hidden = (gate / (1.0 + jnp.exp(-gate)) * up).astype(BF16)
    loads[5].wait()

    def down(first, width):
        def body(j, carry):
            cols = pl.ds(pl.multiple_of(first + j * step, step), step)
            part[:, :, cols] = dot(hidden, w_out[:, cols]).astype(BF16).reshape(N, 16, step)
            return carry

        lax.fori_loop(0, width // step, body, 0)

    over = {}

    def hand_over(*blocks):
        for d in blocks:
            over[d] = start(remote(
                part.at[block(d), :, own_cols(mine=False)], rung.at[block(d)],
                rr_sem, (len(over),), at(x, y + 1 - 2 * side),
            ))

    down((1 - side) * (own_w + both_w), own_w)
    hand_over(HALF, HALF - 1, 1 - HALF)

    def scatter_copy(piece, way, hop, src):
        is_own, first, width = pieces[piece]
        if hop == 1:
            width //= 2
        dst = (got_own if is_own else got_both).at[way, hop - 1, :, first : first + width]
        return remote(src, dst, s_sem, (piece, way, hop - 1), at(x + 1 - 2 * way, y))

    scatters = {}
    down(own_w, both_w)
    for piece in range(len(pieces)):
        if piece not in own_pieces:
            half = pieces[piece][2] // 2
            for way in range(2):
                src = part.at[block(HALF), :, piece_cols(piece, way * half, half)]
                scatters[piece, way, 1] = start(scatter_copy(piece, way, 1, src))
    down(side * (own_w + both_w), own_w)

    def mine(piece, d):
        is_own, first, width = pieces[piece]
        value = part[block(d), :, piece_cols(piece)].astype(F32)
        if is_own:
            value = value + rung[block(d), :, first : first + width].astype(F32)
        return value

    over[HALF].wait_recv()
    for piece in own_pieces:
        first, half = pieces[piece][1], pieces[piece][2] // 2
        send_own[0, 0, :, first : first + 2 * half] = mine(piece, HALF).astype(BF16)
        for way in range(2):
            src = send_own.at[0, 0, :, first + way * half : first + (way + 1) * half]
            scatters[piece, way, 1] = start(scatter_copy(piece, way, 1, src))
    hand_over(2, -2)
    for hop in range(2, HALF + 1):
        if hop == 2:
            hand_over(1, -1)
        if hop == 3:
            hand_over(0)
        arrived = set()
        for piece in [i for i in range(len(pieces)) if i not in own_pieces] + own_pieces:
            is_own, first, width = pieces[piece]
            send, got = (send_own, got_own) if is_own else (send_both, got_both)
            for way in range(2):
                d = (1 - 2 * way) * (HALF + 1 - hop)
                if is_own and d not in arrived:
                    over[d].wait_recv()
                    arrived.add(d)
                scatters[piece, way, hop - 1].wait_recv()
                value = mine(piece, d)
                if hop == 2:
                    half = width // 2
                    halves = [value[:, :half], value[:, half:]]
                    halves[way] = halves[way] + got[way, 0, :, first : first + half].astype(F32)
                    value = jnp.concatenate(halves, axis=1)
                else:
                    value = value + got[way, hop - 2, :, first : first + width].astype(F32)
                send[way, hop - 1, :, first : first + width] = value.astype(BF16)
                src = send.at[way, hop - 1, :, first : first + width]
                scatters[piece, way, hop] = start(scatter_copy(piece, way, hop, src))

    last_copies = []
    for is_own in (False, True):
        got, last, landing, sems = (
            (got_own, last_own, own_ref, lo_sem) if is_own else (got_both, last_both, both_ref, lb_sem)
        )
        if is_own:
            over[0].wait_recv()
        values = []
        for piece, (kind, first, width) in enumerate(pieces):
            if kind == is_own:
                value = mine(piece, 0)
                for way in range(2):
                    scatters[piece, way, HALF].wait_recv()
                    value = value + got[way, HALF - 1, :, first : first + width].astype(F32)
                values.append(value.astype(BF16))
        value = jnp.concatenate(values, axis=1)
        for k in range(own_units if is_own else both_units):
            stacked = jnp.concatenate(
                [value[:, k * UNIT + i * LANES : k * UNIT + (i + 1) * LANES] for i in range(8)], axis=0
            )
            last[:, k] = dot(scatter_perm, stacked).astype(BF16).reshape(N, 16, LANES)
        for d in range(N):
            to_y = lax.rem(y + d, N)
            last_copies.append(start(remote(
                last.at[to_y], landing.at[expert, side], sems, (d,), {**ahead, **at(x, to_y)},
            )))

    for d in range(1, reps):

        @pl.when(rep + d < reps)
        def _():
            mass_copy(d, d).wait_recv()
            mass_copy(reps + d, d).start()

    pw_copy.wait_recv()
    for copy in last_copies:
        copy.wait_recv()
    for d in range(1, reps):

        @pl.when(rep - d >= 0)
        def _():
            mass_copy(reps + d, -d).wait_recv()
            mass_copy(d, -d).wait_send()

    for d in range(1, reps):

        @pl.when(rep + d < reps)
        def _():
            mass_copy(reps + d, d).wait_send()

    keep.wait()
    for copy in sent:
        copy.wait_send()


def spread_kernel(
    count, pw_hbm, mass_hbm, both_hbm, own_hbm, handed_hbm, share_ref, pw, mass, both, own, out, in_sem, out_sem
):
    pairs = ((pw_hbm, pw), (mass_hbm, mass), (both_hbm, both), (own_hbm, own))
    loads = [pltpu.make_async_copy(src, dst, in_sem.at[i]) for i, (src, dst) in enumerate(pairs)]
    for load in loads:
        load.start()
    tokens = pw.shape[1]
    own_units, both_units = own.shape[2], both.shape[2]
    copy_row = one_hot(iota((8 * tokens, tokens), 1) == lax.rem(iota((8 * tokens, tokens), 0), tokens))

    def widen(picks):
        wide = lax.dot_general(copy_row, picks, (((1,), (1,)), ((), ())), preferred_element_type=F32)
        wide_rows, wide_cols = iota(wide.shape, 0), iota(wide.shape, 1)
        return jnp.where(lax.rem(wide_cols, 8) == lax.div(wide_rows, tokens), wide, 0.0).astype(BF16)

    loads[0].wait()
    wide_one = widen(pw[...])
    wide_two = widen(jnp.concatenate([pw[e * 16 : e * 16 + 16] for e in range(EXPERTS) for _ in range(2)], axis=0))
    loads[1].wait()
    load = functools.reduce(jnp.add, [mass[i] for i in range(mass.shape[0])])
    lane, row = iota((8, LANES), 1), iota((8, LANES), 0)
    share_ref[...] = jnp.sum(jnp.where(lane == row, load, 0.0), axis=0, keepdims=True)[:, :EXPERTS] / count
    outs = []

    def spread(wide, first, values):
        value = jnp.concatenate(values, axis=1)
        tall = dot(wide, value).astype(BF16)
        for k in range(len(values)):
            for i in range(8):
                column = (first + k) * UNIT + i * LANES
                out[:, column : column + LANES] = tall[i * tokens : (i + 1) * tokens, k * LANES : (k + 1) * LANES]
        cols = pl.ds(first * UNIT, len(values) * UNIT)
        copy = pltpu.make_async_copy(out.at[:, cols], handed_hbm.at[:, cols], out_sem.at[len(outs)])
        copy.start()
        outs.append(copy)

    loads[2].wait()
    spread(wide_two, own_units, [both[:, :, k].reshape(EXPERTS * 32, LANES) for k in range(both_units)])
    loads[3].wait()
    for half in range(2):
        spread(
            wide_one, half * (own_units + both_units),
            [own[:, half, k].reshape(EXPERTS * 16, LANES) for k in range(own_units)],
        )
    for copy in outs:
        copy.wait()


def local(activations, routes, gate_values, w_gate, w_up, w_down):
    acts = activations[0, 0]
    tokens, width = acts.shape
    sections, reps = lax.axis_size("section"), lax.axis_size("rep")
    own_units = width // UNIT * 2 // 7
    both_units = width // UNIT - 2 * own_units
    own_w, both_w = own_units * UNIT, both_units * UNIT
    pieces = (
        (True, 0, own_w // 2), (False, 0, both_w // 2), (True, own_w // 2, own_w // 2), (False, both_w // 2, both_w // 2)
    )
    vmem = pl.BlockSpec(memory_space=pltpu.VMEM)
    hbm = pl.BlockSpec(memory_space=pl.ANY)
    dma = pltpu.SemaphoreType.DMA
    count = float(reps * lax.axis_size("expert") * tokens)
    own_shape = (EXPERTS, 2, own_units, 16, LANES)
    both_shape = (EXPERTS, 2, both_units, 16, LANES)
    pw_shape = (EXPERTS * 16, tokens)
    mass_shape = (reps, 8, LANES)
    own, both, pw, mass = pl.pallas_call(
        functools.partial(layer_kernel, (sections, reps, own_units, both_units, pieces)),
        out_shape=(
            jax.ShapeDtypeStruct(own_shape, BF16),
            jax.ShapeDtypeStruct(both_shape, BF16),
            jax.ShapeDtypeStruct(pw_shape, BF16),
            jax.ShapeDtypeStruct(mass_shape, F32),
        ),
        in_specs=[hbm] * 6,
        out_specs=(hbm,) * 4,
        scratch_shapes=[
            pltpu.VMEM(routes.shape[:1:-1], jnp.int32),
            pltpu.VMEM(routes.shape[:1:-1], F32),
            pltpu.VMEM((tokens, width), BF16),
            pltpu.VMEM((width, 2 * LANES), BF16),
            pltpu.VMEM((LANES, width), BF16),
            pltpu.VMEM((EXPERTS, 2 * own_units + both_units, 16, LANES), BF16),
            pltpu.VMEM((N, own_units, 16, LANES), BF16),
            pltpu.VMEM((N, both_units, 16, LANES), BF16),
            pltpu.VMEM((N, 16, width), BF16),
            pltpu.VMEM((EXPERTS * 16, tokens), BF16),
            pltpu.VMEM((3, 8, LANES), F32),
            pltpu.VMEM((N, 8, LANES), F32),
            pltpu.VMEM((N, 8, LANES), F32),
            pltpu.VMEM((N, 16, width), BF16),
            pltpu.VMEM((N, 16, own_w), BF16),
            pltpu.VMEM((2, HALF, 16, own_w), BF16),
            pltpu.VMEM((2, HALF, 16, both_w), BF16),
            pltpu.VMEM((2, HALF, 16, own_w), BF16),
            pltpu.VMEM((2, HALF, 16, both_w), BF16),
            pltpu.VMEM((N, own_units, 16, LANES), BF16),
            pltpu.VMEM((N, both_units, 16, LANES), BF16),
            dma((6,)),
            dma((2,)),
            dma((2, N)),
            dma((2, N)),
            dma((2, 2 * reps)),
            dma((2, N)),
            dma((2, N)),
            dma((2, len(pieces), 2, HALF)),
            dma((2, (N + 1) * len(pieces))),
            dma((2, N)),
            dma((2, len(pieces), 2, HALF)),
            dma((2, N)),
            dma((2, N)),
            dma,
        ],
        compiler_params=pltpu.CompilerParams(
            collective_id=0, has_side_effects=True, vmem_limit_bytes=60 * 2**20
        ),
        name="layer",
    )(routes[0, 0].T, gate_values[0, 0].T, acts, w_gate[0], w_up[0], w_down[0])
    handed, share = pl.pallas_call(
        functools.partial(spread_kernel, count),
        out_shape=(
            jax.ShapeDtypeStruct((tokens, width), BF16),
            jax.ShapeDtypeStruct((1, EXPERTS), F32),
        ),
        in_specs=[hbm] * 4,
        out_specs=(hbm, vmem),
        scratch_shapes=[
            pltpu.VMEM(pw_shape, BF16),
            pltpu.VMEM(mass_shape, F32),
            pltpu.VMEM(both_shape, BF16),
            pltpu.VMEM(own_shape, BF16),
            pltpu.VMEM((tokens, width), BF16),
            dma((4,)),
            dma((3,)),
        ],
        compiler_params=pltpu.CompilerParams(vmem_limit_bytes=60 * 2**20),
        name="spread",
    )(pw, mass, both, own)
    return handed[None, None], share


def solution(mesh):
    placed = (
        P("section", "rep", "expert", None),
        P("section", "rep", "expert", None),
        P("section", "rep", "expert", None),
        P("section", None, "expert"),
        P("section", None, "expert"),
        P("section", "expert", None),
    )
    return jax.shard_map(
        local,
        mesh=mesh,
        in_specs=placed,
        out_specs=(P("section", "rep", "expert", None), P("section", None)),
        check_vma=False,
    )
```

```python
import functools

import jax
import jax.numpy as jnp
from jax import lax
from jax.experimental import pallas as pl
from jax.experimental.pallas import tpu as pltpu
from jax.sharding import PartitionSpec as P

MESH = pl.DeviceIdType.MESH
BF16 = jnp.bfloat16
F32 = jnp.float32
EXPERTS = 4
N = 8
HALF = N // 2
UNIT = 1024
LANES = 128


def iota(shape, axis):
    return lax.broadcasted_iota(jnp.int32, shape, axis)


def dot(a, b):
    return jnp.dot(a, b, preferred_element_type=F32)


def one_hot(mask):
    return jnp.where(mask, 1.0, 0.0).astype(BF16)


def routing(routes_ref, gates_ref):
    tokens = routes_ref.shape[1]
    rows = EXPERTS * 2 * 8
    row = iota((rows, tokens), 0)
    expert = lax.div(row, 16)
    slot = lax.rem(lax.div(row, 8), 2).astype(F32)
    hits = jnp.zeros((rows, tokens), F32)
    mass = jnp.zeros((rows, tokens), F32)
    for k in range(routes_ref.shape[0]):
        same = routes_ref[k : k + 1, :] == expert
        hits = hits + jnp.where(same, 1.0, 0.0)
        mass = mass + jnp.where(same, gates_ref[k : k + 1, :], 0.0)
    earlier = one_hot(iota((tokens, tokens), 0) < iota((tokens, tokens), 1))
    before = dot(hits.astype(BF16), earlier)
    picks = jnp.where(before == slot, hits, 0.0)
    return picks, mass


def expert_mass(routes_ref, gates_ref):
    tokens = routes_ref.shape[1]
    expert = iota((8, tokens), 0)
    mass = jnp.zeros((8, tokens), F32)
    for k in range(routes_ref.shape[0]):
        same = routes_ref[k : k + 1, :] == expert
        mass = mass + jnp.where(same, gates_ref[k : k + 1, :], 0.0)
    return jnp.broadcast_to(jnp.sum(mass, axis=1, keepdims=True), (8, LANES))


def layer_kernel(
    sizes,
    routes_hbm, gates_hbm, acts_hbm, gate_hbm, up_hbm, down_hbm,
    own_ref, both_ref, pw_ref, mass_z,
    routes_ref, gates_ref,
    acts, w_in, w_out, picked, first_own, first_both, rows, pw_out,
    mass_out, mass_y, mass_x,
    part, rung, send_own, send_both, got_own, got_both, last_own, last_both,
    load_sem, pw_sem, my_sem, mx_sem, mz_sem, fo_sem, fb_sem,
    g_sem, gr_sem, rr_sem, s_sem, lo_sem, lb_sem, keep_sem,
):
    sections, reps, own_units, both_units, pieces = sizes
    own_w, both_w = own_units * UNIT, both_units * UNIT
    tokens = acts.shape[0]
    section, rep, index = (lax.axis_index(a) for a in ("section", "rep", "expert"))
    x, y = lax.rem(index, N), lax.div(index, N)
    expert, side = lax.div(y, 2), lax.rem(y, 2)

    def at(x_, y_):
        return {"expert": lax.rem(y_ + N, N) * N + lax.rem(x_ + N, N)}

    def block(d):
        return lax.rem(x + d + N, N)

    def remote(src, dst, sems, i, device):
        return pltpu.make_async_remote_copy(
            src_ref=src, dst_ref=dst, send_sem=sems.at[(0, *i)], recv_sem=sems.at[(1, *i)],
            device_id=device, device_id_type=MESH,
        )

    sent, older = [], []

    def set_aside():
        older.extend(sent)
        sent.clear()

    def drain():
        for copy in older:
            copy.wait_send()
        older.clear()

    def start(copy):
        copy.start()
        sent.append(copy)
        return copy

    def finish():
        for copy in sent:
            copy.wait_send()

    loads = [
        pltpu.make_async_copy(routes_hbm, routes_ref, load_sem.at[0]),
        pltpu.make_async_copy(gates_hbm, gates_ref, load_sem.at[1]),
        pltpu.make_async_copy(acts_hbm, acts, load_sem.at[2]),
        pltpu.make_async_copy(gate_hbm, w_in.at[:, 0:LANES], load_sem.at[3]),
        pltpu.make_async_copy(up_hbm, w_in.at[:, LANES : 2 * LANES], load_sem.at[4]),
        pltpu.make_async_copy(down_hbm, w_out, load_sem.at[5]),
    ]
    for load in loads[:3]:
        load.start()

    ahead = {"section": lax.rem(section + 1, sections)}
    behind = {"section": lax.rem(section + sections - 1, sections)}
    barrier = pltpu.get_barrier_semaphore()
    for d in range(1, N):
        for device in (at(x, y + d - N), at(x + d - N, y)):
            pl.semaphore_signal(barrier, inc=1, device_id=device, device_id_type=MESH)
    for d in range(1, reps):

        @pl.when(rep + d < reps)
        def _():
            pl.semaphore_signal(barrier, inc=1, device_id={"rep": rep + d}, device_id_type=MESH)

    for d in range(N):
        pl.semaphore_signal(barrier, inc=1, device_id={**behind, **at(x, y + d - N)}, device_id_type=MESH)

    loads[0].wait()
    loads[1].wait()
    picks, mass = routing(routes_ref, gates_ref)
    pw_out[...] = jnp.where(picks > 0, mass, 0.0).astype(BF16)
    mass_out[0] = expert_mass(routes_ref, gates_ref)
    spread = one_hot(iota((tokens, 8 * tokens), 0) == lax.rem(iota((tokens, 8 * tokens), 1), tokens))
    wide = dot(picks.astype(BF16), spread)
    wide_rows, wide_cols = iota(wide.shape, 0), iota(wide.shape, 1)
    wide = jnp.where(lax.rem(wide_rows, 8) == lax.div(wide_cols, tokens), wide, 0.0).astype(BF16)
    loads[2].wait()

    def pick_unit(u):
        stacked = jnp.concatenate(
            [acts[:, u * UNIT + i * LANES : u * UNIT + (i + 1) * LANES] for i in range(8)], axis=0
        )
        picked[:, u] = dot(wide, stacked).astype(BF16).reshape(EXPERTS, 16, LANES)

    for u in (*range(own_units), *range(own_units + both_units, 2 * own_units + both_units)):
        pick_unit(u)
    pl.semaphore_wait(barrier, (N - 1) * 2 + N + rep)

    own_copies, both_copies, mass_copies = [], [], []
    for d in range(1, N):
        to_y = lax.rem(y + d, N)
        own_copies.append(start(remote(
            picked.at[lax.div(to_y, 2), pl.ds(lax.rem(to_y, 2) * (own_units + both_units), own_units)],
            first_own.at[y], fo_sem, (d,), at(x, to_y),
        )))
    for load in loads[3:]:
        load.start()
    first_own[y] = picked[expert, pl.ds(side * (own_units + both_units), own_units)]
    for u in range(own_units, own_units + both_units):
        pick_unit(u)
    for d in range(1, N):
        to_y = lax.rem(y + d, N)
        both_copies.append(start(remote(
            picked.at[lax.div(to_y, 2), pl.ds(own_units, both_units)],
            first_both.at[y], fb_sem, (d,), at(x, to_y),
        )))
    first_both[y] = picked[expert, pl.ds(own_units, both_units)]
    pw_copy = start(remote(pw_out, pw_ref, pw_sem, (), {**ahead}))
    for d in range(1, N):
        mass_copies.append(start(remote(mass_out.at[0], mass_y.at[y], my_sem, (d,), at(x, y + d - N))))
    mass_y[y] = mass_out[0]

    perm_rows, perm_cols = iota((128, 128), 0), iota((128, 128), 1)

    def inner(k):
        return lax.rem(lax.div(k, 2), 8) * 16 + lax.rem(k, 2) * 8 + lax.div(k, 16)

    gather_perm = one_hot(perm_cols == inner(perm_rows))
    scatter_perm = one_hot(perm_rows == inner(perm_cols))

    def assemble(buf, k):
        mixed = dot(gather_perm, buf[:, k].reshape(128, LANES)).astype(BF16)
        return jnp.concatenate([mixed[i * 16 : (i + 1) * 16] for i in range(8)], axis=1)

    def own_cols(first=0, width=own_w, mine=True):
        which = side if mine else 1 - side
        return pl.ds(pl.multiple_of(which * (own_w + both_w) + first, LANES), width)

    def both_cols(first=0, width=both_w):
        return pl.ds(own_w + first, width)

    def piece_cols(piece, first=0, width=None):
        is_own, start_, width_ = pieces[piece]
        cols = own_cols if is_own else both_cols
        return cols(start_ + first, width or width_)

    own_pieces = [i for i, piece in enumerate(pieces) if piece[0]]

    def gather_copy(piece, way, hop):
        sign = 1 if way == 0 else -1
        width = pieces[piece][2]
        first = 0
        if hop == HALF:
            width //= 2
            first = way * width
        ref = rows.at[block(-sign * (hop - 1)), :, piece_cols(piece, first, width)]
        return remote(ref, ref, g_sem, (piece, way, hop - 1), at(x + sign, y))

    def rung_copy(i, d, piece, first=0, width=None):
        ref = rows.at[block(d), :, piece_cols(piece, first, width)]
        return remote(ref, ref, gr_sem, (i,), at(x, y + 1 - 2 * side))

    gathers = {}
    rungs = []
    for copy in own_copies:
        copy.wait_recv()
    for k in range(own_units):
        rows[x, :, own_cols(k * UNIT, UNIT)] = assemble(first_own, k)
    for piece in own_pieces:
        for way in range(2):
            gathers[piece, way, 1] = start(gather_copy(piece, way, 1))
        rungs.append(start(rung_copy(len(rungs), 0, piece)))
    for copy in both_copies:
        copy.wait_recv()
    for k in range(both_units):
        rows[x, :, both_cols(k * UNIT, UNIT)] = assemble(first_both, k)
    for piece in range(len(pieces)):
        if piece not in own_pieces:
            for way in range(2):
                gathers[piece, way, 1] = start(gather_copy(piece, way, 1))

    def mass_copy(i, d):
        return remote(mass_out.at[2], mass_z.at[rep], mz_sem, (i,), {"rep": rep + d})

    keep = pltpu.make_async_copy(mass_out.at[2], mass_z.at[rep], keep_sem)

    for copy in mass_copies:
        copy.wait_recv()
    mass_out[1] = functools.reduce(jnp.add, [mass_y[i] for i in range(N)])
    mass_x[x] = mass_out[1]
    mass_copies = [
        start(remote(mass_out.at[1], mass_x.at[x], mx_sem, (d,), at(x + d - N, y))) for d in range(1, N)
    ]

    for hop in range(1, HALF):
        for piece in range(len(pieces)):
            for way in range(2):
                gathers[piece, way, hop].wait_recv()
                gathers[piece, way, hop + 1] = start(gather_copy(piece, way, hop + 1))
                if piece in own_pieces:
                    rungs.append(start(rung_copy(len(rungs), (-1 if way == 0 else 1) * hop, piece)))
        if hop == 1:
            for copy in mass_copies:
                copy.wait_recv()
            mass_out[2] = functools.reduce(jnp.add, [mass_x[i] for i in range(N)])
            keep.start()
            for d in range(1, reps):

                @pl.when(rep - d >= 0)
                def _():
                    mass_copy(d, -d).start()

    for piece in own_pieces:
        for way in range(2):
            gathers[piece, way, HALF].wait_recv()
            width = pieces[piece][2] // 2
            rungs.append(start(rung_copy(len(rungs), HALF, piece, way * width, width)))

    step = 512

    def project(total, first, width):
        def body(j, total):
            cols = pl.ds(pl.multiple_of(first + j * step, step), step)
            return total + dot(rows[:, :, cols].reshape(128, step), w_in[cols, :])

        return lax.fori_loop(0, width // step, body, total)

    loads[3].wait()
    loads[4].wait()
    total = project(jnp.zeros((128, 2 * LANES), F32), side * (own_w + both_w), own_w)
    for piece in range(len(pieces)):
        if piece not in own_pieces:
            for way in range(2):
                gathers[piece, way, HALF].wait_recv()
    total = project(total, own_w, both_w)
    for copy in rungs:
        copy.wait_recv()
    total = project(total, (1 - side) * (own_w + both_w), own_w)
    gate, up = total[:, :LANES], total[:, LANES:]
    hidden = (gate / (1.0 + jnp.exp(-gate)) * up).astype(BF16)
    loads[5].wait()

    def down(first, width):
        def body(j, carry):
            cols = pl.ds(pl.multiple_of(first + j * step, step), step)
            part[:, :, cols] = dot(hidden, w_out[:, cols]).astype(BF16).reshape(N, 16, step)
            return carry

        lax.fori_loop(0, width // step, body, 0)

    set_aside()

    over = {}

    def hand_over(*blocks):
        for d in blocks:
            over[d] = start(remote(
                part.at[block(d), :, own_cols(mine=False)], rung.at[block(d)],
                rr_sem, (len(over),), at(x, y + 1 - 2 * side),
            ))

    down((1 - side) * (own_w + both_w), own_w)
    hand_over(HALF, HALF - 1, 1 - HALF)

    def scatter_copy(piece, way, hop, src):
        is_own, first, width = pieces[piece]
        if hop == 1:
            width //= 2
        dst = (got_own if is_own else got_both).at[way, hop - 1, :, first : first + width]
        return remote(src, dst, s_sem, (piece, way, hop - 1), at(x + 1 - 2 * way, y))

    scatters = {}
    down(own_w, both_w)
    for piece in range(len(pieces)):
        if piece not in own_pieces:
            half = pieces[piece][2] // 2
            for way in range(2):
                src = part.at[block(HALF), :, piece_cols(piece, way * half, half)]
                scatters[piece, way, 1] = start(scatter_copy(piece, way, 1, src))
    down(side * (own_w + both_w), own_w)

    def mine(piece, d):
        is_own, first, width = pieces[piece]
        value = part[block(d), :, piece_cols(piece)].astype(F32)
        if is_own:
            value = value + rung[block(d), :, first : first + width].astype(F32)
        return value

    over[HALF].wait_recv()
    for piece in own_pieces:
        first, half = pieces[piece][1], pieces[piece][2] // 2
        send_own[0, 0, :, first : first + 2 * half] = mine(piece, HALF).astype(BF16)
        for way in range(2):
            src = send_own.at[0, 0, :, first + way * half : first + (way + 1) * half]
            scatters[piece, way, 1] = start(scatter_copy(piece, way, 1, src))
    hand_over(2, -2)
    drain()
    for hop in range(2, HALF + 1):
        if hop == 2:
            hand_over(1, -1)
        if hop == 3:
            hand_over(0)
        if hop == HALF:
            set_aside()
        arrived = set()
        for piece in [i for i in range(len(pieces)) if i not in own_pieces] + own_pieces:
            is_own, first, width = pieces[piece]
            send, got = (send_own, got_own) if is_own else (send_both, got_both)
            for way in range(2):
                d = (1 - 2 * way) * (HALF + 1 - hop)
                if is_own and d not in arrived:
                    over[d].wait_recv()
                    arrived.add(d)
                scatters[piece, way, hop - 1].wait_recv()
                value = mine(piece, d)
                if hop == 2:
                    half = width // 2
                    halves = [value[:, :half], value[:, half:]]
                    halves[way] = halves[way] + got[way, 0, :, first : first + half].astype(F32)
                    value = jnp.concatenate(halves, axis=1)
                else:
                    value = value + got[way, hop - 2, :, first : first + width].astype(F32)
                send[way, hop - 1, :, first : first + width] = value.astype(BF16)
                src = send.at[way, hop - 1, :, first : first + width]
                scatters[piece, way, hop] = start(scatter_copy(piece, way, hop, src))

    drain()

    last_copies = []
    for is_own in (False, True):
        got, last, landing, sems = (
            (got_own, last_own, own_ref, lo_sem) if is_own else (got_both, last_both, both_ref, lb_sem)
        )
        if is_own:
            over[0].wait_recv()
        values = []
        for piece, (kind, first, width) in enumerate(pieces):
            if kind == is_own:
                value = mine(piece, 0)
                for way in range(2):
                    scatters[piece, way, HALF].wait_recv()
                    value = value + got[way, HALF - 1, :, first : first + width].astype(F32)
                values.append(value.astype(BF16))
        value = jnp.concatenate(values, axis=1)
        for k in range(own_units if is_own else both_units):
            stacked = jnp.concatenate(
                [value[:, k * UNIT + i * LANES : k * UNIT + (i + 1) * LANES] for i in range(8)], axis=0
            )
            last[:, k] = dot(scatter_perm, stacked).astype(BF16).reshape(N, 16, LANES)
        for d in range(N):
            to_y = lax.rem(y + d, N)
            last_copies.append(start(remote(
                last.at[to_y], landing.at[expert, side], sems, (d,), {**ahead, **at(x, to_y)},
            )))

    for d in range(1, reps):

        @pl.when(rep + d < reps)
        def _():
            mass_copy(d, d).wait_recv()
            mass_copy(reps + d, d).start()

    pw_copy.wait_recv()
    for copy in last_copies:
        copy.wait_recv()
    for d in range(1, reps):

        @pl.when(rep - d >= 0)
        def _():
            mass_copy(reps + d, -d).wait_recv()
            mass_copy(d, -d).wait_send()

    for d in range(1, reps):

        @pl.when(rep + d < reps)
        def _():
            mass_copy(reps + d, d).wait_send()

    keep.wait()
    for copy in sent:
        copy.wait_send()


def spread_kernel(
    count, pw_hbm, mass_hbm, both_hbm, own_hbm, handed_hbm, share_ref, pw, mass, both, own, out, in_sem, out_sem
):
    pairs = ((pw_hbm, pw), (mass_hbm, mass), (both_hbm, both), (own_hbm, own))
    loads = [pltpu.make_async_copy(src, dst, in_sem.at[i]) for i, (src, dst) in enumerate(pairs)]
    for load in loads:
        load.start()
    tokens = pw.shape[1]
    own_units, both_units = own.shape[2], both.shape[2]
    copy_row = one_hot(iota((8 * tokens, tokens), 1) == lax.rem(iota((8 * tokens, tokens), 0), tokens))

    def widen(picks):
        wide = lax.dot_general(copy_row, picks, (((1,), (1,)), ((), ())), preferred_element_type=F32)
        wide_rows, wide_cols = iota(wide.shape, 0), iota(wide.shape, 1)
        return jnp.where(lax.rem(wide_cols, 8) == lax.div(wide_rows, tokens), wide, 0.0).astype(BF16)

    loads[0].wait()
    wide_one = widen(pw[...])
    wide_two = widen(jnp.concatenate([pw[e * 16 : e * 16 + 16] for e in range(EXPERTS) for _ in range(2)], axis=0))
    loads[1].wait()
    load = functools.reduce(jnp.add, [mass[i] for i in range(mass.shape[0])])
    lane, row = iota((8, LANES), 1), iota((8, LANES), 0)
    share_ref[...] = jnp.sum(jnp.where(lane == row, load, 0.0), axis=0, keepdims=True)[:, :EXPERTS] / count
    outs = []

    def spread(wide, first, values):
        value = jnp.concatenate(values, axis=1)
        tall = dot(wide, value).astype(BF16)
        for k in range(len(values)):
            for i in range(8):
                column = (first + k) * UNIT + i * LANES
                out[:, column : column + LANES] = tall[i * tokens : (i + 1) * tokens, k * LANES : (k + 1) * LANES]
        cols = pl.ds(first * UNIT, len(values) * UNIT)
        copy = pltpu.make_async_copy(out.at[:, cols], handed_hbm.at[:, cols], out_sem.at[len(outs)])
        copy.start()
        outs.append(copy)

    loads[2].wait()
    spread(wide_two, own_units, [both[:, :, k].reshape(EXPERTS * 32, LANES) for k in range(both_units)])
    loads[3].wait()
    for half in range(2):
        spread(
            wide_one, half * (own_units + both_units),
            [own[:, half, k].reshape(EXPERTS * 16, LANES) for k in range(own_units)],
        )
    for copy in outs:
        copy.wait()


def local(activations, routes, gate_values, w_gate, w_up, w_down):
    acts = activations[0, 0]
    tokens, width = acts.shape
    sections, reps = lax.axis_size("section"), lax.axis_size("rep")
    own_units = width // UNIT * 2 // 7
    both_units = width // UNIT - 2 * own_units
    own_w, both_w = own_units * UNIT, both_units * UNIT
    pieces = (
        (True, 0, own_w // 2), (False, 0, both_w // 2), (True, own_w // 2, own_w // 2), (False, both_w // 2, both_w // 2)
    )
    vmem = pl.BlockSpec(memory_space=pltpu.VMEM)
    hbm = pl.BlockSpec(memory_space=pl.ANY)
    dma = pltpu.SemaphoreType.DMA
    count = float(reps * lax.axis_size("expert") * tokens)
    own_shape = (EXPERTS, 2, own_units, 16, LANES)
    both_shape = (EXPERTS, 2, both_units, 16, LANES)
    pw_shape = (EXPERTS * 16, tokens)
    mass_shape = (reps, 8, LANES)
    own, both, pw, mass = pl.pallas_call(
        functools.partial(layer_kernel, (sections, reps, own_units, both_units, pieces)),
        out_shape=(
            jax.ShapeDtypeStruct(own_shape, BF16),
            jax.ShapeDtypeStruct(both_shape, BF16),
            jax.ShapeDtypeStruct(pw_shape, BF16),
            jax.ShapeDtypeStruct(mass_shape, F32),
        ),
        in_specs=[hbm] * 6,
        out_specs=(hbm,) * 4,
        scratch_shapes=[
            pltpu.VMEM(routes.shape[:1:-1], jnp.int32),
            pltpu.VMEM(routes.shape[:1:-1], F32),
            pltpu.VMEM((tokens, width), BF16),
            pltpu.VMEM((width, 2 * LANES), BF16),
            pltpu.VMEM((LANES, width), BF16),
            pltpu.VMEM((EXPERTS, 2 * own_units + both_units, 16, LANES), BF16),
            pltpu.VMEM((N, own_units, 16, LANES), BF16),
            pltpu.VMEM((N, both_units, 16, LANES), BF16),
            pltpu.VMEM((N, 16, width), BF16),
            pltpu.VMEM((EXPERTS * 16, tokens), BF16),
            pltpu.VMEM((3, 8, LANES), F32),
            pltpu.VMEM((N, 8, LANES), F32),
            pltpu.VMEM((N, 8, LANES), F32),
            pltpu.VMEM((N, 16, width), BF16),
            pltpu.VMEM((N, 16, own_w), BF16),
            pltpu.VMEM((2, HALF, 16, own_w), BF16),
            pltpu.VMEM((2, HALF, 16, both_w), BF16),
            pltpu.VMEM((2, HALF, 16, own_w), BF16),
            pltpu.VMEM((2, HALF, 16, both_w), BF16),
            pltpu.VMEM((N, own_units, 16, LANES), BF16),
            pltpu.VMEM((N, both_units, 16, LANES), BF16),
            dma((6,)),
            dma((2,)),
            dma((2, N)),
            dma((2, N)),
            dma((2, 2 * reps)),
            dma((2, N)),
            dma((2, N)),
            dma((2, len(pieces), 2, HALF)),
            dma((2, (N + 1) * len(pieces))),
            dma((2, N)),
            dma((2, len(pieces), 2, HALF)),
            dma((2, N)),
            dma((2, N)),
            dma,
        ],
        compiler_params=pltpu.CompilerParams(
            collective_id=0, has_side_effects=True, vmem_limit_bytes=60 * 2**20
        ),
        name="layer",
    )(routes[0, 0].T, gate_values[0, 0].T, acts, w_gate[0], w_up[0], w_down[0])
    handed, share = pl.pallas_call(
        functools.partial(spread_kernel, count),
        out_shape=(
            jax.ShapeDtypeStruct((tokens, width), BF16),
            jax.ShapeDtypeStruct((1, EXPERTS), F32),
        ),
        in_specs=[hbm] * 4,
        out_specs=(hbm, vmem),
        scratch_shapes=[
            pltpu.VMEM(pw_shape, BF16),
            pltpu.VMEM(mass_shape, F32),
            pltpu.VMEM(both_shape, BF16),
            pltpu.VMEM(own_shape, BF16),
            pltpu.VMEM((tokens, width), BF16),
            dma((4,)),
            dma((3,)),
        ],
        compiler_params=pltpu.CompilerParams(vmem_limit_bytes=60 * 2**20),
        name="spread",
    )(pw, mass, both, own)
    return handed[None, None], share


def solution(mesh):
    placed = (
        P("section", "rep", "expert", None),
        P("section", "rep", "expert", None),
        P("section", "rep", "expert", None),
        P("section", None, "expert"),
        P("section", None, "expert"),
        P("section", "expert", None),
    )
    return jax.shard_map(
        local,
        mesh=mesh,
        in_specs=placed,
        out_specs=(P("section", "rep", "expert", None), P("section", None)),
        check_vma=False,
    )
```
